32 devices in a mesh: pole: 2 (over x), prow: 16 (over z, y, core).
Axes of the slice: x: 2, y: 2, z: 4, core: 2. Of those that a mesh axis runs over, the one named last changes fastest.
Arguments:
- factor_blocks: bfloat16 [256, 4, 128, 128], P(('pole', 'prow')), parts along dimension 0, may hold values from -0.25 to 0.25
- inverse_blocks: bfloat16 [64, 32, 128, 128], P(('pole', 'prow')), parts along dimension 0, may hold values from -6 to 6
- diag_factor_inv: float32 [256, 128, 128], P(('pole', 'prow')), parts along dimension 0, may hold values from -6 to 6
- structure: int32 [128, 4], replicated, may hold values from 0 to 31, all different within a row; in each aligned block of 8 rows (0 to 7, 8 to 15, ...) no two rows name the same one
Outputs:
- diag_inverse: float32 [256, 128, 128], P(('pole', 'prow')), parts along dimension 0
The draws below stay inside these ranges and needn't reach their ends.
There are 2 independent parts, one for each index of `pole`. The reference program is written for one: setup_inputs(seed, part) draws one part's arguments, and reference() takes and returns one part's arrays. A program takes and returns all parts, laid end to end along the dimension named above; an argument that names none is the same for every part. Nothing has to cross between parts.
Inputs may be any that keep to these rules, and one draw needn't show every extreme that they name: `structure`: the 4 entries of a row are distinct, and within the rows of one device (aligned blocks of 8 rows) no ancestor is named twice; every ancestor is named by some row.
All inputs are finite; a program needn't handle non-finite values.
Results may differ from the reference program's by a relative error of at most 0.0021.
Values may be sent and summed in bfloat16 or wider, within the bound.
No kernel may reach another device: no remote copies, remote signals or barrier semaphores. Data moves between devices by JAX's collectives and lax.ppermute only.
A program may use at most 128 MiB of HBM per device.

```python
import math
import jax
import jax.numpy as jnp
import numpy as np
from jax import lax

B = 128
R = 4
KDEV = 8
S = 128
M = 32


def shard_levels(stream_key, shape, cuts, least, high):
    def one(axis_at, shards_of):
        steps = jax.random.uniform(jax.random.fold_in(jax.random.fold_in(stream_key, 6), axis_at), (shards_of,), jnp.float32, least / len(cuts), high / len(cuts))
        return jnp.repeat(jnp.exp(steps), shape[axis_at] // shards_of).reshape((-1,) + (1,) * (len(shape) - axis_at - 1))

    factor_of = one(*cuts[0])
    for cut in cuts[1:]:
        factor_of = factor_of * one(*cut)
    return factor_of


def routed_block(stream_key, own, number, rows, amount, top, most, slope):
    sequence = jax.random.permutation(stream_key, amount)
    heavy_load, ordinary = portions_of(amount, rows * top, most, slope, True), portions_of(amount, rows * top, most, slope, False)
    places = jnp.arange(amount)

    def named(tallies, turn):
        used = int((tallies > 0).sum())
        fixed = max(1, used // 4)
        shifted = fixed + (places - fixed + turn * (used - fixed)) % max(1, amount - fixed)
        return jnp.zeros((amount,), jnp.int32).at[sequence[jnp.where(places < fixed, places, shifted)]].set(jnp.asarray(tallies, jnp.int32))

    tallies = jnp.where(number % 4 == 0, named(heavy_load, number // 4), named(ordinary, number - number // 4 - 1))
    mixed = jax.random.permutation(jax.random.fold_in(own, 3), amount)
    source_of, taker = mixed[0:amount // 2 * 2:2], mixed[1:amount // 2 * 2:2]
    room = jnp.minimum(tallies[source_of] - 1, most - tallies[taker]) // 2
    room = jnp.where((source_of == sequence[0]) | (taker == sequence[0]) | (tallies[taker] == 0), 0, jnp.maximum(room, 0))
    shifted = jax.random.randint(jax.random.fold_in(own, 4), (amount // 2,), 0, 1 << 20) % (room + 1)
    tallies = tallies.at[source_of].add(-shifted).at[taker].add(shifted)
    members = jnp.searchsorted(jnp.cumsum(tallies), jnp.arange(rows * top), side="right").astype(jnp.int32)
    table = members.reshape(top, rows).T
    table = table[jax.random.permutation(jax.random.fold_in(own, 1), rows)]
    turn = jax.random.randint(jax.random.fold_in(own, 2), (rows, 1), 0, top)
    return jnp.take_along_axis(table, (jnp.arange(top)[None, :] + turn) % top, axis=1)


def portions_of(count, total, limit, lean, full):
    portions = [(1 << 20) // math.isqrt(grade ** lean) + 1 for grade in range(1, count + 1)]
    largest = limit if full else min(limit, max(-(-total // count), total * portions[0] // sum(portions)))
    least = 1 if total - largest >= count - 1 else 0
    given, spare = [largest] + [least] * (count - 1), total - largest - least * (count - 1)
    while spare > 0:
        candidates = [i for i in range(1, count) if given[i] < largest] or [i for i in range(1, count) if given[i] < limit]
        mass, left = sum([portions[i] for i in candidates]), spare
        for i in candidates:
            more = min(limit - given[i], max(1, left * portions[i] // mass), spare)
            given[i] = given[i] + more
            spare = spare - more
    return np.array(given)


def bell_draw(rng, dims, deviation, bound, shards=(), dtype=jnp.bfloat16):
    factor_of = shard_levels(rng, dims, shards, -0.22, 0.18) if shards else 1.0
    values = jax.random.normal(rng, dims, jnp.float32) * deviation * factor_of
    return jnp.minimum(jnp.maximum(values, -bound), bound).astype(dtype)


def setup_inputs(seed: int = 0, part: int = 0) -> dict:
    arg_keys = jax.random.split(jax.random.key(seed), 5)
    part_splits = jax.random.split(jax.random.fold_in(arg_keys[4], part), 5)
    factor_blocks = bell_draw(part_splits[0], (S, R, B, B), (R * B) ** -0.5, 0.25, ((0, 16),))
    inverse_blocks = bell_draw(part_splits[1], (M, M, B, B), 1.0, 6.0, ((0, 16),))
    diag_factor_inv = bell_draw(part_splits[2], (S, B, B), 1.0, 6.0, ((0, 16),), jnp.float32)
    structure_keys = jax.random.split(jax.random.fold_in(arg_keys[3], 1), S // KDEV)
    structure_turns = jax.random.permutation(jax.random.fold_in(arg_keys[3], 3), S // KDEV)
    structure = jax.vmap(lambda own, number: routed_block(jax.random.fold_in(arg_keys[3], 2), own, number, KDEV, M, R, 1, 2))(structure_keys, structure_turns).reshape((S, R))
    return dict(factor_blocks=factor_blocks, inverse_blocks=inverse_blocks, diag_factor_inv=diag_factor_inv, structure=structure)


def reference(factor_blocks, inverse_blocks, diag_factor_inv, structure):
    def column_term(items):
        rows_list, factor = items
        blocks = inverse_blocks[rows_list[:, None], rows_list[None, :]]
        product = jnp.einsum("rsxy,syz->rxz", blocks.astype(jnp.float32), factor.astype(jnp.float32))
        product = product.astype(jnp.bfloat16)
        return jnp.einsum("rix,riz->xz", factor.astype(jnp.float32), product.astype(jnp.float32))

    summed = lax.map(column_term, (structure, factor_blocks))
    return diag_factor_inv + summed
```

```python
import functools

import jax
import jax.numpy as jnp
from jax import lax
from jax.experimental import pallas as pl
from jax.experimental.pallas import tpu as pltpu
from jax.sharding import PartitionSpec as P


def pack_kernel(n, cols, me_ref, st_ref, inv_ref, send_ref, diag_ref, idx_v, idx_s, sem, sem_d, sem_i):
    length, total = st_ref.shape
    rows = inv_ref.shape[0]
    others = length - 1
    me = me_ref[0]
    for j in range(rows):
        pltpu.make_async_copy(inv_ref.at[j, me * rows + j], diag_ref.at[j], sem_d).start()
    st = [st_ref[r : r + 1, :] for r in range(length)]
    lines = []
    for j in range(rows):
        row = me * rows + j
        for q in range(others):
            line = jnp.zeros((1, total), jnp.int32)
            for r in range(length):
                s = q if q < r else q + 1
                line = jnp.where(st[r] == row, st[s], line)
            lines.append(line)
    pad = idx_v.shape[0] - len(lines)
    lines.append(jnp.zeros((pad, total), jnp.int32))
    picks = jnp.concatenate(lines, axis=0).astype(jnp.float32)
    first = lax.broadcasted_iota(jnp.int32, (total, idx_v.shape[1]), 1) * cols
    place = lax.broadcasted_iota(jnp.int32, (total, idx_v.shape[1]), 0)
    group = ((place >= first) & (place < first + cols)).astype(jnp.float32)
    table = jnp.dot(picks, group, preferred_element_type=jnp.float32, precision=lax.Precision.HIGHEST)
    idx_v[...] = table.astype(jnp.int32)
    copy = pltpu.make_async_copy(idx_v, idx_s, sem_i)
    copy.start()
    copy.wait()

    def to_device(p, carry):
        for j in range(rows):
            for q in range(others):
                c = idx_s[j * others + q, p]
                pltpu.make_async_copy(inv_ref.at[j, c], send_ref.at[p, j, q], sem).start()
        return carry

    lax.fori_loop(0, n, to_device, 0)
    pltpu.make_async_copy(diag_ref, diag_ref, sem_d).wait()
    pltpu.make_async_copy(send_ref, send_ref, sem).wait()


def level_kernel(me_ref, st_ref, recv_ref, diag_ref, fac_ref, dfi_ref, out_ref, mat, sems):
    cols = fac_ref.shape[0]
    width = out_ref.shape[1]
    length = fac_ref.shape[1] // width
    rows = diag_ref.shape[1]
    me = me_ref[0]

    for k in range(cols):
        for r in range(length):
            anc = st_ref[(me * cols + k) * length + r]
            owner = lax.div(anc, rows)
            local = lax.rem(anc, rows)
            here = pl.ds(r * width, width)
            for s in range(length):
                if s == r:
                    src = diag_ref.at[lax.bitwise_xor(owner, me), local]
                else:
                    src = recv_ref.at[owner, local, s if s < r else s - 1]
                pltpu.make_async_copy(src, mat.at[k, here, pl.ds(s * width, width)], sems.at[k]).start()
    for k in range(cols):
        pltpu.make_async_copy(mat.at[k], mat.at[k], sems.at[k]).wait()
        fac = fac_ref[k]
        product = jnp.dot(mat[k], fac, preferred_element_type=jnp.float32).astype(jnp.bfloat16)
        term = lax.dot_general(fac, product, (((0,), (0,)), ((), ())), preferred_element_type=jnp.float32)
        out_ref[k] = dfi_ref[k] + term


def shards(n, factor_blocks, inverse_blocks, diag_factor_inv, structure):
    cols, length, width, _ = factor_blocks.shape
    rows, ancestors = inverse_blocks.shape[:2]
    total = structure.shape[0]
    me = lax.axis_index("prow").astype(jnp.int32)
    me1 = me.reshape(1)
    smem = pl.BlockSpec(memory_space=pltpu.SMEM)
    vmem = pl.BlockSpec(memory_space=pltpu.VMEM)
    hbm = pl.BlockSpec(memory_space=pl.ANY)
    lines = -(-rows * (length - 1) // 8) * 8
    lanes = -(-n // 128) * 128
    send, diag = pl.pallas_call(
        functools.partial(pack_kernel, n, cols),
        out_shape=(
            jax.ShapeDtypeStruct((n, rows, length - 1, width, width), jnp.bfloat16),
            jax.ShapeDtypeStruct((rows, width, width), jnp.bfloat16),
        ),
        in_specs=[smem, vmem, hbm],
        out_specs=(hbm, hbm),
        scratch_shapes=[
            pltpu.VMEM((lines, lanes), jnp.int32),
            pltpu.SMEM((lines, lanes), jnp.int32),
            pltpu.SemaphoreType.DMA,
            pltpu.SemaphoreType.DMA,
            pltpu.SemaphoreType.DMA,
        ],
    )(me1, structure.T, inverse_blocks)
    recv = lax.all_to_all(send, "prow", split_axis=0, concat_axis=0, tiled=True)
    held = diag.reshape(1, rows, width, width)
    mask = 1
    while mask < n:
        came = lax.ppermute(held, "prow", [(i, i ^ mask) for i in range(n)])
        held = jnp.concatenate([held, came], axis=0)
        mask *= 2
    return pl.pallas_call(
        level_kernel,
        out_shape=jax.ShapeDtypeStruct((cols, width, width), jnp.float32),
        in_specs=[smem, smem, hbm, hbm, vmem, vmem],
        out_specs=vmem,
        scratch_shapes=[
            pltpu.VMEM((cols, length * width, length * width), jnp.bfloat16),
            pltpu.SemaphoreType.DMA((cols,)),
        ],
        compiler_params=pltpu.CompilerParams(vmem_limit_bytes=32 * 2**20),
    )(me1, structure.reshape(-1), recv, held, factor_blocks.reshape(cols, length * width, width), diag_factor_inv)


def solution(mesh):
    placed = (
        P(("pole", "prow"), None, None, None),
        P(("pole", "prow"), None, None, None),
        P(("pole", "prow"), None, None),
        P(),
    )
    return jax.shard_map(
        functools.partial(shards, mesh.shape["prow"]),
        mesh=mesh,
        in_specs=placed,
        out_specs=P(("pole", "prow"), None, None),
        check_vma=False,
    )
```

```python
import functools

import jax
import jax.numpy as jnp
from jax import lax
from jax.experimental import pallas as pl
from jax.experimental.pallas import tpu as pltpu
from jax.sharding import PartitionSpec as P


def diag_kernel(me_ref, inv_ref, diag_ref, sem):
    rows = inv_ref.shape[0]
    for j in range(rows):
        pltpu.make_async_copy(inv_ref.at[j, me_ref[0] * rows + j], diag_ref.at[0, j], sem.at[j]).start()
    for j in range(rows):
        pltpu.make_async_copy(inv_ref.at[j, 0], diag_ref.at[0, j], sem.at[j]).wait()


def pack_kernel(n, cols, me_ref, st_ref, inv_ref, send_ref, send_v, idx_v, idx_s, sem_i, sem_o):
    length, total = st_ref.shape
    rows = inv_ref.shape[0]
    others = length - 1
    me = me_ref[0]
    st = [st_ref[r : r + 1, :] for r in range(length)]
    lines = []
    for j in range(rows):
        row = me * rows + j
        for q in range(others):
            line = jnp.zeros((1, total), jnp.int32)
            for r in range(length):
                line = jnp.where(st[r] == row, st[q if q < r else q + 1], line)
            lines.append(line)
    lines.append(jnp.zeros((idx_v.shape[0] - len(lines), total), jnp.int32))
    picks = jnp.concatenate(lines, axis=0).astype(jnp.float32)
    grid = (total, idx_v.shape[1])
    first = lax.broadcasted_iota(jnp.int32, grid, 1) * cols
    place = lax.broadcasted_iota(jnp.int32, grid, 0)
    group = ((place >= first) & (place < first + cols)).astype(jnp.float32)
    table = jnp.dot(picks, group, preferred_element_type=jnp.float32, precision=lax.Precision.HIGHEST)
    idx_v[...] = table.astype(jnp.int32)
    copy = pltpu.make_async_copy(idx_v, idx_s, sem_i)
    copy.start()
    copy.wait()

    def to_device(p, carry):
        for j in range(rows):
            for q in range(others):
                send_v[p, j, q] = inv_ref[j, idx_s[j * others + q, p]]
        pltpu.make_async_copy(send_v.at[p], send_ref.at[p], sem_o).start()
        return carry

    lax.fori_loop(0, n, to_device, 0)
    pltpu.make_async_copy(send_v, send_ref, sem_o).wait()


def level_kernel(quad, me_ref, st_ref, recv_ref, *rest):
    diag_refs, rest = rest[:quad], rest[quad:]
    fac_ref, dfi_ref, out_ref, diag_v, fac_v, dfi_v, out_v, sems, sem_d, sem_g, sem_o = rest
    cols, deep, width = fac_v.shape
    length = deep // width
    rows = recv_ref.shape[1]
    steps = diag_refs[0].shape[0]
    me = me_ref[0]
    for a in range(quad):
        for t in range(steps):
            owner = lax.bitwise_xor(lax.rem(me + t * quad, steps * quad), a)
            pltpu.make_async_copy(diag_refs[a].at[t], diag_v.at[pl.ds(owner * rows, rows)], sem_g).start()
    fetch = [pltpu.make_async_copy(fac_ref.at[k], fac_v.at[k], sems.at[k]) for k in range(cols)]
    fetch_d = pltpu.make_async_copy(dfi_ref, dfi_v, sem_d)
    for f in fetch:
        f.start()
    fetch_d.start()
    pltpu.make_async_copy(diag_v, diag_v, sem_g).wait()
    for k in range(cols):
        fetch[k].wait()
        fac = fac_v[k]
        product = []
        for r in range(length):
            anc = st_ref[r, me * cols + k]
            owner, local = lax.div(anc, rows), lax.rem(anc, rows)
            line = [diag_v[anc] if s == r else recv_ref[owner, local, s if s < r else s - 1] for s in range(length)]
            line = jnp.concatenate(line, axis=1)
            product.append(jnp.dot(line, fac, preferred_element_type=jnp.float32).astype(jnp.bfloat16))
        product = jnp.concatenate(product, axis=0)
        term = lax.dot_general(fac, product, (((0,), (0,)), ((), ())), preferred_element_type=jnp.float32)
        if k == 0:
            fetch_d.wait()
        out_v[k] = dfi_v[k] + term
        pltpu.make_async_copy(out_v.at[k], out_ref.at[k], sem_o).start()
    pltpu.make_async_copy(out_v, out_ref, sem_o).wait()


def shards(n, factor_blocks, inverse_blocks, diag_factor_inv, structure):
    cols, length, width, _ = factor_blocks.shape
    rows, ancestors = inverse_blocks.shape[:2]
    total = structure.shape[0]
    me = lax.axis_index("prow").astype(jnp.int32)
    me1 = me.reshape(1)
    smem = pl.BlockSpec(memory_space=pltpu.SMEM)
    vmem = pl.BlockSpec(memory_space=pltpu.VMEM)
    hbm = pl.BlockSpec(memory_space=pltpu.HBM)
    quad = 4
    steps = n // quad

    diag = pl.pallas_call(
        diag_kernel,
        out_shape=jax.ShapeDtypeStruct((1, rows, width, width), jnp.bfloat16),
        in_specs=[smem, hbm],
        out_specs=vmem,
        scratch_shapes=[pltpu.SemaphoreType.DMA((rows,))],
    )(me1, inverse_blocks)
    held = [diag]
    for t in range(1, steps):
        held.append(lax.ppermute(diag, "prow", [((i + t * quad) % n, i) for i in range(n)]))
    held = jnp.concatenate(held, axis=0)
    lines = -(-rows * (length - 1) // 8) * 8
    lanes = -(-n // 128) * 128
    send = pl.pallas_call(
        functools.partial(pack_kernel, n, cols),
        out_shape=jax.ShapeDtypeStruct((n, rows, length - 1, width, width), jnp.bfloat16),
        in_specs=[smem, vmem, vmem],
        out_specs=hbm,
        scratch_shapes=[
            pltpu.VMEM((n, rows, length - 1, width, width), jnp.bfloat16),
            pltpu.VMEM((lines, lanes), jnp.int32),
            pltpu.SMEM((lines, lanes), jnp.int32),
            pltpu.SemaphoreType.DMA,
            pltpu.SemaphoreType.DMA,
        ],
        compiler_params=pltpu.CompilerParams(vmem_limit_bytes=40 * 2**20),
    )(me1, structure.T, inverse_blocks)
    send, held = lax.optimization_barrier((send, held))
    spread = [held]
    for a in range(1, quad):
        spread.append(lax.ppermute(held, "prow", [(i ^ a, i) for i in range(n)]))
    recv = lax.all_to_all(send, "prow", split_axis=0, concat_axis=0, tiled=True)
    deep = length * width
    return pl.pallas_call(
        functools.partial(level_kernel, quad),
        out_shape=jax.ShapeDtypeStruct((cols, width, width), jnp.float32),
        in_specs=[smem, smem, vmem] + [hbm] * (quad + 2),
        out_specs=hbm,
        scratch_shapes=[
            pltpu.VMEM((ancestors, width, width), jnp.bfloat16),
            pltpu.VMEM((cols, deep, width), jnp.bfloat16),
            pltpu.VMEM((cols, width, width), jnp.float32),
            pltpu.VMEM((cols, width, width), jnp.float32),
            pltpu.SemaphoreType.DMA((cols,)),
            pltpu.SemaphoreType.DMA,
            pltpu.SemaphoreType.DMA,
            pltpu.SemaphoreType.DMA,
        ],
        compiler_params=pltpu.CompilerParams(vmem_limit_bytes=48 * 2**20),
    )(me1, structure.T, recv, *spread, factor_blocks.reshape(cols, deep, width), diag_factor_inv)


def solution(mesh):
    placed = (
        P(("pole", "prow"), None, None, None),
        P(("pole", "prow"), None, None, None),
        P(("pole", "prow"), None, None),
        P(),
    )
    return jax.shard_map(
        functools.partial(shards, mesh.shape["prow"]),
        mesh=mesh,
        in_specs=placed,
        out_specs=P(("pole", "prow"), None, None),
        check_vma=False,
    )
```

```python
import functools

import jax
import jax.numpy as jnp
from jax import lax
from jax.experimental import pallas as pl
from jax.experimental.pallas import tpu as pltpu
from jax.sharding import PartitionSpec as P


def pack_kernel(n, cols, me_ref, st_ref, inv_ref, send_ref, diag_ref, inv_v, send_v, idx_v, idx_s, sem, sem_i, sem_d, sem_o):
    length, total = st_ref.shape
    rows = inv_ref.shape[0]
    others = length - 1
    me = me_ref[0]
    fetch = pltpu.make_async_copy(inv_ref, inv_v, sem)
    fetch.start()
    st = [st_ref[r : r + 1, :] for r in range(length)]
    lines = []
    for j in range(rows):
        row = me * rows + j
        for q in range(others):
            line = jnp.zeros((1, total), jnp.int32)
            for r in range(length):
                line = jnp.where(st[r] == row, st[q if q < r else q + 1], line)
            lines.append(line)
    lines.append(jnp.zeros((idx_v.shape[0] - len(lines), total), jnp.int32))
    picks = jnp.concatenate(lines, axis=0).astype(jnp.float32)
    grid = (total, idx_v.shape[1])
    first = lax.broadcasted_iota(jnp.int32, grid, 1) * cols
    place = lax.broadcasted_iota(jnp.int32, grid, 0)
    group = ((place >= first) & (place < first + cols)).astype(jnp.float32)
    table = jnp.dot(picks, group, preferred_element_type=jnp.float32, precision=lax.Precision.HIGHEST)
    idx_v[...] = table.astype(jnp.int32)
    copy = pltpu.make_async_copy(idx_v, idx_s, sem_i)
    copy.start()
    copy.wait()
    fetch.wait()
    for j in range(rows):
        pltpu.make_async_copy(inv_v.at[j, me * rows + j], diag_ref.at[0, j], sem_d).start()

    def to_device(p, carry):
        for j in range(rows):
            for q in range(others):
                send_v[p, j, q] = inv_v[j, idx_s[j * others + q, p]]
        pltpu.make_async_copy(send_v.at[p], send_ref.at[p], sem_o).start()
        return carry

    lax.fori_loop(0, n, to_device, 0)
    pltpu.make_async_copy(send_v, send_ref, sem_o).wait()
    pltpu.make_async_copy(diag_ref, diag_ref, sem_d).wait()


def level_kernel(quad, me_ref, st_ref, recv_ref, *rest):
    diag_refs, rest = rest[:quad], rest[quad:]
    fac_ref, dfi_ref, out_ref, diag_v, line_v, out_v, sems, sem_o = rest
    cols, deep, width = fac_ref.shape
    length = deep // width
    rows = recv_ref.shape[1]
    steps = diag_refs[0].shape[0]
    me = me_ref[0]
    for k in range(cols):
        for r in range(length):
            anc = st_ref[r, me * cols + k]
            src = recv_ref.at[lax.div(anc, rows), lax.rem(anc, rows)]
            pltpu.make_async_copy(src, line_v.at[k, r], sems.at[k]).start()
    for a in range(quad):
        for t in range(steps):
            owner = lax.bitwise_xor(lax.rem(me + t * quad, steps * quad), a)
            diag_v[pl.ds(owner * rows, rows)] = diag_refs[a][t]
    for k in range(cols):
        fac = fac_ref[k]
        pltpu.make_async_copy(line_v.at[k], line_v.at[k], sems.at[k]).wait()
        product = []
        for r in range(length):
            anc = st_ref[r, me * cols + k]
            line = [diag_v[anc] if s == r else line_v[k, r, s if s < r else s - 1] for s in range(length)]
            line = jnp.concatenate(line, axis=1)
            product.append(jnp.dot(line, fac, preferred_element_type=jnp.float32).astype(jnp.bfloat16))
        product = jnp.concatenate(product, axis=0)
        term = lax.dot_general(fac, product, (((0,), (0,)), ((), ())), preferred_element_type=jnp.float32)
        out_v[k] = dfi_ref[k] + term
        pltpu.make_async_copy(out_v.at[k], out_ref.at[k], sem_o).start()
    pltpu.make_async_copy(out_v, out_ref, sem_o).wait()


def shards(n, factor_blocks, inverse_blocks, diag_factor_inv, structure):
    cols, length, width, _ = factor_blocks.shape
    rows, ancestors = inverse_blocks.shape[:2]
    total = structure.shape[0]
    me = lax.axis_index("prow").astype(jnp.int32)
    me1 = me.reshape(1)
    smem = pl.BlockSpec(memory_space=pltpu.SMEM)
    vmem = pl.BlockSpec(memory_space=pltpu.VMEM)
    hbm = pl.BlockSpec(memory_space=pltpu.HBM)
    quad = 4
    steps = n // quad

    lines = -(-rows * (length - 1) // 8) * 8
    lanes = -(-n // 128) * 128
    send, diag = pl.pallas_call(
        functools.partial(pack_kernel, n, cols),
        out_shape=(
            jax.ShapeDtypeStruct((n, rows, length - 1, width, width), jnp.bfloat16),
            jax.ShapeDtypeStruct((1, rows, width, width), jnp.bfloat16),
        ),
        in_specs=[smem, vmem, hbm],
        out_specs=(hbm, hbm),
        scratch_shapes=[
            pltpu.VMEM(inverse_blocks.shape, jnp.bfloat16),
            pltpu.VMEM((n, rows, length - 1, width, width), jnp.bfloat16),
            pltpu.VMEM((lines, lanes), jnp.int32),
            pltpu.SMEM((lines, lanes), jnp.int32),
            pltpu.SemaphoreType.DMA,
            pltpu.SemaphoreType.DMA,
            pltpu.SemaphoreType.DMA,
            pltpu.SemaphoreType.DMA,
        ],
        compiler_params=pltpu.CompilerParams(vmem_limit_bytes=56 * 2**20),
    )(me1, structure.T, inverse_blocks)
    recv = lax.all_to_all(send, "prow", split_axis=0, concat_axis=0, tiled=True)
    held = [diag]
    for t in range(1, steps):
        held.append(lax.ppermute(diag, "prow", [((i + t * quad) % n, i) for i in range(n)]))
    held = jnp.concatenate(held, axis=0)
    spread = [held]
    for a in range(1, quad):
        spread.append(lax.ppermute(held, "prow", [(i ^ a, i) for i in range(n)]))
    deep = length * width
    return pl.pallas_call(
        functools.partial(level_kernel, quad),
        out_shape=jax.ShapeDtypeStruct((cols, width, width), jnp.float32),
        in_specs=[smem, smem, hbm] + [vmem] * (quad + 2),
        out_specs=hbm,
        scratch_shapes=[
            pltpu.VMEM((ancestors, width, width), jnp.bfloat16),
            pltpu.VMEM((cols, length, length - 1, width, width), jnp.bfloat16),
            pltpu.VMEM((cols, width, width), jnp.float32),
            pltpu.SemaphoreType.DMA((cols,)),
            pltpu.SemaphoreType.DMA,
        ],
        compiler_params=pltpu.CompilerParams(vmem_limit_bytes=51 * 2**20),
    )(me1, structure.T, recv, *spread, factor_blocks.reshape(cols, deep, width), diag_factor_inv)


def solution(mesh):
    placed = (
        P(("pole", "prow"), None, None, None),
        P(("pole", "prow"), None, None, None),
        P(("pole", "prow"), None, None),
        P(),
    )
    return jax.shard_map(
        functools.partial(shards, mesh.shape["prow"]),
        mesh=mesh,
        in_specs=placed,
        out_specs=P(("pole", "prow"), None, None),
        check_vma=False,
    )
```

```python
import functools

import jax
import jax.numpy as jnp
from jax import lax
from jax.experimental import pallas as pl
from jax.experimental.pallas import tpu as pltpu
from jax.sharding import PartitionSpec as P


def diag_kernel(me_ref, inv_ref, diag_ref, sem):
    rows = inv_ref.shape[0]
    for j in range(rows):
        pltpu.make_async_copy(inv_ref.at[j, me_ref[0] * rows + j], diag_ref.at[0, j], sem.at[j]).start()
    for j in range(rows):
        pltpu.make_async_copy(inv_ref.at[j, 0], diag_ref.at[0, j], sem.at[j]).wait()


def pack_kernel(n, cols, me_ref, st_ref, inv_ref, send_ref, send_v, idx_v, idx_s, sem_i, sem_o):
    length, total = st_ref.shape
    rows = inv_ref.shape[0]
    others = length - 1
    me = me_ref[0]
    st = [st_ref[r : r + 1, :] for r in range(length)]
    lines = []
    for j in range(rows):
        row = me * rows + j
        for q in range(others):
            line = jnp.zeros((1, total), jnp.int32)
            for r in range(length):
                line = jnp.where(st[r] == row, st[q if q < r else q + 1], line)
            lines.append(line)
    lines.append(jnp.zeros((idx_v.shape[0] - len(lines), total), jnp.int32))
    picks = jnp.concatenate(lines, axis=0).astype(jnp.float32)
    grid = (total, idx_v.shape[1])
    first = lax.broadcasted_iota(jnp.int32, grid, 1) * cols
    place = lax.broadcasted_iota(jnp.int32, grid, 0)
    group = ((place >= first) & (place < first + cols)).astype(jnp.float32)
    table = jnp.dot(picks, group, preferred_element_type=jnp.float32, precision=lax.Precision.HIGHEST)
    idx_v[...] = table.astype(jnp.int32)
    copy = pltpu.make_async_copy(idx_v, idx_s, sem_i)
    copy.start()
    copy.wait()

    def to_device(p, carry):
        for j in range(rows):
            for q in range(others):
                send_v[p, j, q] = inv_ref[j, idx_s[j * others + q, p]]
        pltpu.make_async_copy(send_v.at[p], send_ref.at[p], sem_o).start()
        return carry

    lax.fori_loop(0, n, to_device, 0)
    pltpu.make_async_copy(send_v, send_ref, sem_o).wait()


def level_kernel(quad, me_ref, st_ref, recv_ref, *rest):
    diag_refs, rest = rest[:quad], rest[quad:]
    fac_ref, dfi_ref, out_ref, diag_v, line_v, out_v, sems, sem_o = rest
    cols, deep, width = fac_ref.shape
    length = deep // width
    rows = recv_ref.shape[1]
    steps = diag_refs[0].shape[0]
    me = me_ref[0]
    for k in range(cols):
        for r in range(length):
            anc = st_ref[r, me * cols + k]
            src = recv_ref.at[lax.div(anc, rows), lax.rem(anc, rows)]
            pltpu.make_async_copy(src, line_v.at[k, r], sems.at[k]).start()
    for a in range(quad):
        for t in range(steps):
            owner = lax.bitwise_xor(lax.rem(me + t * quad, steps * quad), a)
            diag_v[pl.ds(owner * rows, rows)] = diag_refs[a][t]
    for k in range(cols):
        fac = fac_ref[k]
        pltpu.make_async_copy(line_v.at[k], line_v.at[k], sems.at[k]).wait()
        product = []
        for r in range(length):
            anc = st_ref[r, me * cols + k]
            line = [diag_v[anc] if s == r else line_v[k, r, s if s < r else s - 1] for s in range(length)]
            line = jnp.concatenate(line, axis=1)
            product.append(jnp.dot(line, fac, preferred_element_type=jnp.float32).astype(jnp.bfloat16))
        product = jnp.concatenate(product, axis=0)
        term = lax.dot_general(fac, product, (((0,), (0,)), ((), ())), preferred_element_type=jnp.float32)
        out_v[k] = dfi_ref[k] + term
        pltpu.make_async_copy(out_v.at[k], out_ref.at[k], sem_o).start()
    pltpu.make_async_copy(out_v, out_ref, sem_o).wait()


def shards(n, factor_blocks, inverse_blocks, diag_factor_inv, structure):
    cols, length, width, _ = factor_blocks.shape
    rows, ancestors = inverse_blocks.shape[:2]
    total = structure.shape[0]
    me = lax.axis_index("prow").astype(jnp.int32)
    me1 = me.reshape(1)
    smem = pl.BlockSpec(memory_space=pltpu.SMEM)
    vmem = pl.BlockSpec(memory_space=pltpu.VMEM)
    hbm = pl.BlockSpec(memory_space=pltpu.HBM)
    quad = 8
    steps = n // quad

    diag = pl.pallas_call(
        diag_kernel,
        out_shape=jax.ShapeDtypeStruct((1, rows, width, width), jnp.bfloat16),
        in_specs=[smem, hbm],
        out_specs=vmem,
        scratch_shapes=[pltpu.SemaphoreType.DMA((rows,))],
    )(me1, inverse_blocks)
    came = [lax.ppermute(diag, "prow", [((i + t * quad) % n, i) for i in range(n)]) for t in range(1, steps)]
    lines = -(-rows * (length - 1) // 8) * 8
    lanes = -(-n // 128) * 128
    send = pl.pallas_call(
        functools.partial(pack_kernel, n, cols),
        out_shape=jax.ShapeDtypeStruct((n, rows, length - 1, width, width), jnp.bfloat16),
        in_specs=[smem, vmem, vmem],
        out_specs=hbm,
        scratch_shapes=[
            pltpu.VMEM((n, rows, length - 1, width, width), jnp.bfloat16),
            pltpu.VMEM((lines, lanes), jnp.int32),
            pltpu.SMEM((lines, lanes), jnp.int32),
            pltpu.SemaphoreType.DMA,
            pltpu.SemaphoreType.DMA,
        ],
        compiler_params=pltpu.CompilerParams(vmem_limit_bytes=40 * 2**20),
    )(me1, structure.T, inverse_blocks)
    send, *came = lax.optimization_barrier((send, *came))
    recv = lax.all_to_all(send, "prow", split_axis=0, concat_axis=0, tiled=True)
    held = [diag] + came
    held = jnp.concatenate(held, axis=0)
    spread = [held]
    for a in range(1, quad):
        spread.append(lax.ppermute(held, "prow", [(i ^ a, i) for i in range(n)]))
    deep = length * width
    return pl.pallas_call(
        functools.partial(level_kernel, quad),
        out_shape=jax.ShapeDtypeStruct((cols, width, width), jnp.float32),
        in_specs=[smem, smem, hbm] + [vmem] * (quad + 2),
        out_specs=hbm,
        scratch_shapes=[
            pltpu.VMEM((ancestors, width, width), jnp.bfloat16),
            pltpu.VMEM((cols, length, length - 1, width, width), jnp.bfloat16),
            pltpu.VMEM((cols, width, width), jnp.float32),
            pltpu.SemaphoreType.DMA((cols,)),
            pltpu.SemaphoreType.DMA,
        ],
        compiler_params=pltpu.CompilerParams(vmem_limit_bytes=51 * 2**20),
    )(me1, structure.T, recv, *spread, factor_blocks.reshape(cols, deep, width), diag_factor_inv)


def solution(mesh):
    placed = (
        P(("pole", "prow"), None, None, None),
        P(("pole", "prow"), None, None, None),
        P(("pole", "prow"), None, None),
        P(),
    )
    return jax.shard_map(
        functools.partial(shards, mesh.shape["prow"]),
        mesh=mesh,
        in_specs=placed,
        out_specs=P(("pole", "prow"), None, None),
        check_vma=False,
    )
```

```python
import functools

import jax
import jax.numpy as jnp
from jax import lax
from jax.experimental import pallas as pl
from jax.experimental.pallas import tpu as pltpu
from jax.sharding import PartitionSpec as P


def diag_kernel(me_ref, inv_ref, diag_ref, sem):
    rows = inv_ref.shape[0]
    for j in range(rows):
        pltpu.make_async_copy(inv_ref.at[j, me_ref[0] * rows + j], diag_ref.at[0, j], sem.at[j]).start()
    for j in range(rows):
        pltpu.make_async_copy(inv_ref.at[j, 0], diag_ref.at[0, j], sem.at[j]).wait()


def pack_kernel(n, cols, me_ref, st_ref, inv_ref, send_ref, send_v, idx_v, idx_s, sem_i, sem_o):
    length, total = st_ref.shape
    rows = inv_ref.shape[0]
    others = length - 1
    me = me_ref[0]
    st = [st_ref[r : r + 1, :] for r in range(length)]
    lines = []
    for j in range(rows):
        row = me * rows + j
        for q in range(others):
            line = jnp.zeros((1, total), jnp.int32)
            for r in range(length):
                line = jnp.where(st[r] == row, st[q if q < r else q + 1], line)
            lines.append(line)
    lines.append(jnp.zeros((idx_v.shape[0] - len(lines), total), jnp.int32))
    picks = jnp.concatenate(lines, axis=0).astype(jnp.float32)
    grid = (total, idx_v.shape[1])
    first = lax.broadcasted_iota(jnp.int32, grid, 1) * cols
    place = lax.broadcasted_iota(jnp.int32, grid, 0)
    group = ((place >= first) & (place < first + cols)).astype(jnp.float32)
    table = jnp.dot(picks, group, preferred_element_type=jnp.float32, precision=lax.Precision.HIGHEST)
    idx_v[...] = table.astype(jnp.int32)
    copy = pltpu.make_async_copy(idx_v, idx_s, sem_i)
    copy.start()
    copy.wait()

    def to_device(p, carry):
        for j in range(rows):
            for q in range(others):
                send_v[p, j, q] = inv_ref[j, idx_s[j * others + q, p]]
        pltpu.make_async_copy(send_v.at[p], send_ref.at[p], sem_o).start()
        return carry

    lax.fori_loop(0, n, to_device, 0)
    pltpu.make_async_copy(send_v, send_ref, sem_o).wait()


def level_kernel(n, quad, me_ref, st_ref, recv_ref, *rest):
    diag_refs, rest = rest[:2], rest[2:]
    fac_ref, dfi_ref, out_ref, diag_v, line_v, out_v, sems, sem_o = rest
    cols, deep, width = fac_ref.shape
    length = deep // width
    rows = recv_ref.shape[1]
    steps = n // quad
    me = me_ref[0]
    count = recv_ref.shape[0]
    parts = sems.shape[0]
    each = count // parts
    fetch = [
        pltpu.make_async_copy(recv_ref.at[pl.ds(i * each, each)], line_v.at[pl.ds(i * each, each)], sems.at[i]) for i in range(parts)
    ]
    for f in fetch:
        f.start()
    for a in range(2):
        for t in range(diag_refs[a].shape[0]):
            owner = lax.bitwise_xor(lax.rem(me + t % steps * quad, n), t // steps * 2 + a)
            diag_v[pl.ds(owner * rows, rows)] = diag_refs[a][t]
    for k in range(cols):
        fac = fac_ref[k]
        if k == 0:
            for f in fetch:
                f.wait()
        product = []
        for r in range(length):
            anc = st_ref[r, me * cols + k]
            line = [diag_v[anc] if s == r else line_v[lax.div(anc, rows), lax.rem(anc, rows), s if s < r else s - 1] for s in range(length)]
            line = jnp.concatenate(line, axis=1)
            product.append(jnp.dot(line, fac, preferred_element_type=jnp.float32).astype(jnp.bfloat16))
        product = jnp.concatenate(product, axis=0)
        term = lax.dot_general(fac, product, (((0,), (0,)), ((), ())), preferred_element_type=jnp.float32)
        out_v[k] = dfi_ref[k] + term
        pltpu.make_async_copy(out_v.at[k], out_ref.at[k], sem_o).start()
    pltpu.make_async_copy(out_v, out_ref, sem_o).wait()


def shards(n, factor_blocks, inverse_blocks, diag_factor_inv, structure):
    cols, length, width, _ = factor_blocks.shape
    rows, ancestors = inverse_blocks.shape[:2]
    total = structure.shape[0]
    me = lax.axis_index("prow").astype(jnp.int32)
    me1 = me.reshape(1)
    smem = pl.BlockSpec(memory_space=pltpu.SMEM)
    vmem = pl.BlockSpec(memory_space=pltpu.VMEM)
    hbm = pl.BlockSpec(memory_space=pltpu.HBM)
    quad = 8
    steps = n // quad

    diag = pl.pallas_call(
        diag_kernel,
        out_shape=jax.ShapeDtypeStruct((1, rows, width, width), jnp.bfloat16),
        in_specs=[smem, hbm],
        out_specs=vmem,
        scratch_shapes=[pltpu.SemaphoreType.DMA((rows,))],
    )(me1, inverse_blocks)
    came = [lax.ppermute(diag, "prow", [((i + t * quad) % n, i) for i in range(n)]) for t in range(1, steps)]
    lines = -(-rows * (length - 1) // 8) * 8
    lanes = -(-n // 128) * 128
    send = pl.pallas_call(
        functools.partial(pack_kernel, n, cols),
        out_shape=jax.ShapeDtypeStruct((n, rows, length - 1, width, width), jnp.bfloat16),
        in_specs=[smem, vmem, vmem],
        out_specs=hbm,
        scratch_shapes=[
            pltpu.VMEM((n, rows, length - 1, width, width), jnp.bfloat16),
            pltpu.VMEM((lines, lanes), jnp.int32),
            pltpu.SMEM((lines, lanes), jnp.int32),
            pltpu.SemaphoreType.DMA,
            pltpu.SemaphoreType.DMA,
        ],
        compiler_params=pltpu.CompilerParams(vmem_limit_bytes=40 * 2**20),
    )(me1, structure.T, inverse_blocks)
    send, *came = lax.optimization_barrier((send, *came))
    recv = lax.all_to_all(send, "prow", split_axis=0, concat_axis=0, tiled=True)
    held = [diag] + came
    held = jnp.concatenate(held, axis=0)
    chips = [held] + [lax.ppermute(held, "prow", [(i ^ a, i) for i in range(n)]) for a in range(2, quad, 2)]
    chips = jnp.concatenate(chips, axis=0)
    spread = [chips, lax.ppermute(chips, "prow", [(i ^ 1, i) for i in range(n)])]
    deep = length * width
    return pl.pallas_call(
        functools.partial(level_kernel, n, quad),
        out_shape=jax.ShapeDtypeStruct((cols, width, width), jnp.float32),
        in_specs=[smem, smem, hbm] + [vmem] * 4,
        out_specs=hbm,
        scratch_shapes=[
            pltpu.VMEM((ancestors, width, width), jnp.bfloat16),
            pltpu.VMEM(recv.shape, jnp.bfloat16),
            pltpu.VMEM((cols, width, width), jnp.float32),
            pltpu.SemaphoreType.DMA((8,)),
            pltpu.SemaphoreType.DMA,
        ],
        compiler_params=pltpu.CompilerParams(vmem_limit_bytes=51 * 2**20),
    )(me1, structure.T, recv, *spread, factor_blocks.reshape(cols, deep, width), diag_factor_inv)


def solution(mesh):
    placed = (
        P(("pole", "prow"), None, None, None),
        P(("pole", "prow"), None, None, None),
        P(("pole", "prow"), None, None),
        P(),
    )
    return jax.shard_map(
        functools.partial(shards, mesh.shape["prow"]),
        mesh=mesh,
        in_specs=placed,
        out_specs=P(("pole", "prow"), None, None),
        check_vma=False,
    )
```

```python
import functools

import jax
import jax.numpy as jnp
from jax import lax
from jax.experimental import pallas as pl
from jax.experimental.pallas import tpu as pltpu
from jax.sharding import PartitionSpec as P


def diag_kernel(me_ref, inv_ref, diag_ref, sem):
    rows = inv_ref.shape[0]
    for j in range(rows):
        pltpu.make_async_copy(inv_ref.at[j, me_ref[0] * rows + j], diag_ref.at[0, j], sem.at[j]).start()
    for j in range(rows):
        pltpu.make_async_copy(inv_ref.at[j, 0], diag_ref.at[0, j], sem.at[j]).wait()


def pack_kernel(n, cols, me_ref, st_ref, inv_ref, send_ref, send_v, idx_v, idx_s, sem_i, sem_o):
    length, total = st_ref.shape
    rows = inv_ref.shape[0]
    others = length - 1
    me = me_ref[0]
    st = [st_ref[r : r + 1, :] for r in range(length)]
    lines = []
    for j in range(rows):
        row = me * rows + j
        for q in range(others):
            line = jnp.zeros((1, total), jnp.int32)
            for r in range(length):
                line = jnp.where(st[r] == row, st[q if q < r else q + 1], line)
            lines.append(line)
    lines.append(jnp.zeros((idx_v.shape[0] - len(lines), total), jnp.int32))
    picks = jnp.concatenate(lines, axis=0).astype(jnp.float32)
    grid = (total, idx_v.shape[1])
    first = lax.broadcasted_iota(jnp.int32, grid, 1) * cols
    place = lax.broadcasted_iota(jnp.int32, grid, 0)
    group = ((place >= first) & (place < first + cols)).astype(jnp.float32)
    table = jnp.dot(picks, group, preferred_element_type=jnp.float32, precision=lax.Precision.HIGHEST)
    idx_v[...] = table.astype(jnp.int32)
    copy = pltpu.make_async_copy(idx_v, idx_s, sem_i)
    copy.start()
    copy.wait()

    def to_device(p, carry):
        for j in range(rows):
            for q in range(others):
                send_v[p, j, q] = inv_ref[j, idx_s[j * others + q, p]]
        pltpu.make_async_copy(send_v.at[p], send_ref.at[p], sem_o).start()
        return carry

    lax.fori_loop(0, n, to_device, 0)
    pltpu.make_async_copy(send_v, send_ref, sem_o).wait()


def level_kernel(n, quad, me_ref, st_ref, recv_ref, *rest):
    diag_refs, rest = rest[:2], rest[2:]
    fac_ref, dfi_ref, out_ref, diag_v, line_v, product_v, out_v, sems, sem_o = rest
    cols, deep, width = fac_ref.shape
    length = deep // width
    rows = recv_ref.shape[1]
    steps = n // quad
    me = me_ref[0]
    count = recv_ref.shape[0]
    parts = sems.shape[0]
    each = count // parts
    fetch = [
        pltpu.make_async_copy(recv_ref.at[pl.ds(i * each, each)], line_v.at[pl.ds(i * each, each)], sems.at[i]) for i in range(parts)
    ]
    for f in fetch:
        f.start()
    for a in range(2):
        for t in range(diag_refs[a].shape[0]):
            owner = lax.bitwise_xor(lax.rem(me + t % steps * quad, n), t // steps * 2 + a)
            diag_v[pl.ds(owner * rows, rows)] = diag_refs[a][t]
    ancs = [[st_ref[r, me * cols + k] for r in range(length)] for k in range(cols)]
    for f in fetch:
        f.wait()
    for k in range(cols):
        for r, anc in enumerate(ancs[k]):
            owner, local = lax.div(anc, rows), lax.rem(anc, rows)
            line = [diag_v[anc] if s == r else line_v[owner, local, s if s < r else s - 1] for s in range(length)]
            line = jnp.concatenate(line, axis=1)
            part = jnp.dot(line, fac_ref[k], preferred_element_type=jnp.float32)
            product_v[k, r * width : (r + 1) * width, :] = part.astype(jnp.bfloat16)
    for k in range(cols):
        term = lax.dot_general(fac_ref[k], product_v[k], (((0,), (0,)), ((), ())), preferred_element_type=jnp.float32)
        out_v[k] = dfi_ref[k] + term
    pltpu.make_async_copy(out_v, out_ref, sem_o).start()
    pltpu.make_async_copy(out_v, out_ref, sem_o).wait()


def shards(n, factor_blocks, inverse_blocks, diag_factor_inv, structure):
    cols, length, width, _ = factor_blocks.shape
    rows, ancestors = inverse_blocks.shape[:2]
    total = structure.shape[0]
    me = lax.axis_index("prow").astype(jnp.int32)
    me1 = me.reshape(1)
    smem = pl.BlockSpec(memory_space=pltpu.SMEM)
    vmem = pl.BlockSpec(memory_space=pltpu.VMEM)
    hbm = pl.BlockSpec(memory_space=pltpu.HBM)
    quad = 8
    steps = n // quad

    diag = pl.pallas_call(
        diag_kernel,
        out_shape=jax.ShapeDtypeStruct((1, rows, width, width), jnp.bfloat16),
        in_specs=[smem, hbm],
        out_specs=vmem,
        scratch_shapes=[pltpu.SemaphoreType.DMA((rows,))],
    )(me1, inverse_blocks)
    came = [lax.ppermute(diag, "prow", [((i + t * quad) % n, i) for i in range(n)]) for t in range(1, steps)]
    lines = -(-rows * (length - 1) // 8) * 8
    lanes = -(-n // 128) * 128
    send = pl.pallas_call(
        functools.partial(pack_kernel, n, cols),
        out_shape=jax.ShapeDtypeStruct((n, rows, length - 1, width, width), jnp.bfloat16),
        in_specs=[smem, vmem, vmem],
        out_specs=hbm,
        scratch_shapes=[
            pltpu.VMEM((n, rows, length - 1, width, width), jnp.bfloat16),
            pltpu.VMEM((lines, lanes), jnp.int32),
            pltpu.SMEM((lines, lanes), jnp.int32),
            pltpu.SemaphoreType.DMA,
            pltpu.SemaphoreType.DMA,
        ],
        compiler_params=pltpu.CompilerParams(vmem_limit_bytes=40 * 2**20),
    )(me1, structure.T, inverse_blocks)
    send, *came = lax.optimization_barrier((send, *came))
    recv = lax.all_to_all(send, "prow", split_axis=0, concat_axis=0, tiled=True)
    held = [diag] + came
    held = jnp.concatenate(held, axis=0)
    chips = [held] + [lax.ppermute(held, "prow", [(i ^ a, i) for i in range(n)]) for a in range(2, quad, 2)]
    chips = jnp.concatenate(chips, axis=0)
    spread = [chips, lax.ppermute(chips, "prow", [(i ^ 1, i) for i in range(n)])]
    deep = length * width
    return pl.pallas_call(
        functools.partial(level_kernel, n, quad),
        out_shape=jax.ShapeDtypeStruct((cols, width, width), jnp.float32),
        in_specs=[smem, smem, hbm] + [vmem] * 4,
        out_specs=hbm,
        scratch_shapes=[
            pltpu.VMEM((ancestors, width, width), jnp.bfloat16),
            pltpu.VMEM(recv.shape, jnp.bfloat16),
            pltpu.VMEM((cols, deep, width), jnp.bfloat16),
            pltpu.VMEM((cols, width, width), jnp.float32),
            pltpu.SemaphoreType.DMA((8,)),
            pltpu.SemaphoreType.DMA,
        ],
        compiler_params=pltpu.CompilerParams(vmem_limit_bytes=51 * 2**20),
    )(me1, structure.T, recv, *spread, factor_blocks.reshape(cols, deep, width), diag_factor_inv)


def solution(mesh):
    placed = (
        P(("pole", "prow"), None, None, None),
        P(("pole", "prow"), None, None, None),
        P(("pole", "prow"), None, None),
        P(),
    )
    return jax.shard_map(
        functools.partial(shards, mesh.shape["prow"]),
        mesh=mesh,
        in_specs=placed,
        out_specs=P(("pole", "prow"), None, None),
        check_vma=False,
    )
```

```python
import functools

import jax
import jax.numpy as jnp
from jax import lax
from jax.experimental import pallas as pl
from jax.experimental.pallas import tpu as pltpu
from jax.sharding import PartitionSpec as P


def diag_kernel(me_ref, inv_ref, diag_ref, sem):
    rows = inv_ref.shape[0]
    for j in range(rows):
        pltpu.make_async_copy(inv_ref.at[j, me_ref[0] * rows + j], diag_ref.at[0, j], sem.at[j]).start()
    for j in range(rows):
        pltpu.make_async_copy(inv_ref.at[j, 0], diag_ref.at[0, j], sem.at[j]).wait()


def pack_kernel(n, cols, me_ref, st_ref, inv_ref, send_ref, inv_v, send_v, idx_v, idx_s, sem, sem_i, sem_o):
    length, total = st_ref.shape
    rows = inv_ref.shape[0]
    others = length - 1
    me = me_ref[0]
    fetch = pltpu.make_async_copy(inv_ref, inv_v, sem)
    fetch.start()
    st = [st_ref[r : r + 1, :] for r in range(length)]
    lines = []
    for j in range(rows):
        row = me * rows + j
        for q in range(others):
            line = jnp.zeros((1, total), jnp.int32)
            for r in range(length):
                line = jnp.where(st[r] == row, st[q if q < r else q + 1], line)
            lines.append(line)
    lines.append(jnp.zeros((idx_v.shape[0] - len(lines), total), jnp.int32))
    picks = jnp.concatenate(lines, axis=0).astype(jnp.float32)
    grid = (total, idx_v.shape[1])
    first = lax.broadcasted_iota(jnp.int32, grid, 1) * cols
    place = lax.broadcasted_iota(jnp.int32, grid, 0)
    group = ((place >= first) & (place < first + cols)).astype(jnp.float32)
    table = jnp.dot(picks, group, preferred_element_type=jnp.float32, precision=lax.Precision.HIGHEST)
    idx_v[...] = table.astype(jnp.int32)
    copy = pltpu.make_async_copy(idx_v, idx_s, sem_i)
    copy.start()
    copy.wait()
    fetch.wait()

    def to_device(p, carry):
        for j in range(rows):
            for q in range(others):
                send_v[p, j, q] = inv_v[j, idx_s[j * others + q, p]]
        pltpu.make_async_copy(send_v.at[p], send_ref.at[p], sem_o).start()
        return carry

    lax.fori_loop(0, n, to_device, 0)
    pltpu.make_async_copy(send_v, send_ref, sem_o).wait()


def level_kernel(n, quad, me_ref, st_ref, recv_ref, *rest):
    diag_refs, rest = rest[:2], rest[2:]
    fac_ref, dfi_ref, out_ref, diag_v, line_v, product_v, out_v, sems, sem_o = rest
    cols, deep, width = fac_ref.shape
    length = deep // width
    rows = recv_ref.shape[1]
    steps = n // quad
    me = me_ref[0]
    count = recv_ref.shape[0]
    parts = sems.shape[0]
    each = count // parts
    fetch = [
        pltpu.make_async_copy(recv_ref.at[pl.ds(i * each, each)], line_v.at[pl.ds(i * each, each)], sems.at[i]) for i in range(parts)
    ]
    for f in fetch:
        f.start()
    for a in range(2):
        for t in range(diag_refs[a].shape[0]):
            owner = lax.bitwise_xor(lax.rem(me + t % steps * quad, n), t // steps * 2 + a)
            diag_v[pl.ds(owner * rows, rows)] = diag_refs[a][t]
    ancs = [[st_ref[r, me * cols + k] for r in range(length)] for k in range(cols)]
    for f in fetch:
        f.wait()
    for k in range(cols):
        for r, anc in enumerate(ancs[k]):
            owner, local = lax.div(anc, rows), lax.rem(anc, rows)
            line = [diag_v[anc] if s == r else line_v[owner, local, s if s < r else s - 1] for s in range(length)]
            line = jnp.concatenate(line, axis=1)
            part = jnp.dot(line, fac_ref[k], preferred_element_type=jnp.float32)
            product_v[k, r * width : (r + 1) * width, :] = part.astype(jnp.bfloat16)
    for k in range(cols):
        term = lax.dot_general(fac_ref[k], product_v[k], (((0,), (0,)), ((), ())), preferred_element_type=jnp.float32)
        out_v[k] = dfi_ref[k] + term
    pltpu.make_async_copy(out_v, out_ref, sem_o).start()
    pltpu.make_async_copy(out_v, out_ref, sem_o).wait()


def shards(n, factor_blocks, inverse_blocks, diag_factor_inv, structure):
    cols, length, width, _ = factor_blocks.shape
    rows, ancestors = inverse_blocks.shape[:2]
    total = structure.shape[0]
    me = lax.axis_index("prow").astype(jnp.int32)
    me1 = me.reshape(1)
    smem = pl.BlockSpec(memory_space=pltpu.SMEM)
    vmem = pl.BlockSpec(memory_space=pltpu.VMEM)
    hbm = pl.BlockSpec(memory_space=pltpu.HBM)
    quad = 8
    steps = n // quad

    diag = pl.pallas_call(
        diag_kernel,
        out_shape=jax.ShapeDtypeStruct((1, rows, width, width), jnp.bfloat16),
        in_specs=[smem, hbm],
        out_specs=vmem,
        scratch_shapes=[pltpu.SemaphoreType.DMA((rows,))],
    )(me1, inverse_blocks)
    came = [lax.ppermute(diag, "prow", [((i + t * quad) % n, i) for i in range(n)]) for t in range(1, steps)]
    lines = -(-rows * (length - 1) // 8) * 8
    lanes = -(-n // 128) * 128
    send = pl.pallas_call(
        functools.partial(pack_kernel, n, cols),
        out_shape=jax.ShapeDtypeStruct((n, rows, length - 1, width, width), jnp.bfloat16),
        in_specs=[smem, vmem, hbm],
        out_specs=hbm,
        scratch_shapes=[
            pltpu.VMEM(inverse_blocks.shape, jnp.bfloat16),
            pltpu.VMEM((n, rows, length - 1, width, width), jnp.bfloat16),
            pltpu.VMEM((lines, lanes), jnp.int32),
            pltpu.SMEM((lines, lanes), jnp.int32),
            pltpu.SemaphoreType.DMA,
            pltpu.SemaphoreType.DMA,
            pltpu.SemaphoreType.DMA,
        ],
        compiler_params=pltpu.CompilerParams(vmem_limit_bytes=56 * 2**20),
    )(me1, structure.T, inverse_blocks)
    send, *came = lax.optimization_barrier((send, *came))
    recv = lax.all_to_all(send, "prow", split_axis=0, concat_axis=0, tiled=True)
    held = [diag] + came
    held = jnp.concatenate(held, axis=0)
    chips = [held] + [lax.ppermute(held, "prow", [(i ^ a, i) for i in range(n)]) for a in range(2, quad, 2)]
    chips = jnp.concatenate(chips, axis=0)
    spread = [chips, lax.ppermute(chips, "prow", [(i ^ 1, i) for i in range(n)])]
    deep = length * width
    return pl.pallas_call(
        functools.partial(level_kernel, n, quad),
        out_shape=jax.ShapeDtypeStruct((cols, width, width), jnp.float32),
        in_specs=[smem, smem, hbm] + [vmem] * 4,
        out_specs=hbm,
        scratch_shapes=[
            pltpu.VMEM((ancestors, width, width), jnp.bfloat16),
            pltpu.VMEM(recv.shape, jnp.bfloat16),
            pltpu.VMEM((cols, deep, width), jnp.bfloat16),
            pltpu.VMEM((cols, width, width), jnp.float32),
            pltpu.SemaphoreType.DMA((8,)),
            pltpu.SemaphoreType.DMA,
        ],
        compiler_params=pltpu.CompilerParams(vmem_limit_bytes=51 * 2**20),
    )(me1, structure.T, recv, *spread, factor_blocks.reshape(cols, deep, width), diag_factor_inv)


def solution(mesh):
    placed = (
        P(("pole", "prow"), None, None, None),
        P(("pole", "prow"), None, None, None),
        P(("pole", "prow"), None, None),
        P(),
    )
    return jax.shard_map(
        functools.partial(shards, mesh.shape["prow"]),
        mesh=mesh,
        in_specs=placed,
        out_specs=P(("pole", "prow"), None, None),
        check_vma=False,
    )
```

```python
import functools

import jax
import jax.numpy as jnp
from jax import lax
from jax.experimental import pallas as pl
from jax.experimental.pallas import tpu as pltpu
from jax.sharding import PartitionSpec as P


def diag_kernel(me_ref, inv_ref, diag_ref, sem):
    rows = inv_ref.shape[0]
    for j in range(rows):
        pltpu.make_async_copy(inv_ref.at[j, me_ref[0] * rows + j], diag_ref.at[0, j], sem.at[j]).start()
    for j in range(rows):
        pltpu.make_async_copy(inv_ref.at[j, 0], diag_ref.at[0, j], sem.at[j]).wait()


def pack_kernel(n, cols, me_ref, st_ref, inv_ref, send_ref, inv_v, send_v, idx_v, idx_s, sem, sem_i, sem_o):
    length, total = st_ref.shape
    rows = inv_ref.shape[0]
    others = length - 1
    me = me_ref[0]
    fetch = pltpu.make_async_copy(inv_ref, inv_v, sem)
    fetch.start()
    st = [st_ref[r : r + 1, :] for r in range(length)]
    lines = []
    for j in range(rows):
        row = me * rows + j
        for q in range(others):
            line = jnp.zeros((1, total), jnp.int32)
            for r in range(length):
                line = jnp.where(st[r] == row, st[q if q < r else q + 1], line)
            lines.append(line)
    lines.append(jnp.zeros((idx_v.shape[0] - len(lines), total), jnp.int32))
    picks = jnp.concatenate(lines, axis=0).astype(jnp.float32)
    grid = (total, idx_v.shape[1])
    first = lax.broadcasted_iota(jnp.int32, grid, 1) * cols
    place = lax.broadcasted_iota(jnp.int32, grid, 0)
    group = ((place >= first) & (place < first + cols)).astype(jnp.float32)
    table = jnp.dot(picks, group, preferred_element_type=jnp.float32, precision=lax.Precision.HIGHEST)
    idx_v[...] = table.astype(jnp.int32)
    copy = pltpu.make_async_copy(idx_v, idx_s, sem_i)
    copy.start()
    copy.wait()
    fetch.wait()

    def to_device(p, carry):
        for j in range(rows):
            for q in range(others):
                send_v[p, j, q] = inv_v[j, idx_s[j * others + q, p]]
        pltpu.make_async_copy(send_v.at[p], send_ref.at[p], sem_o).start()
        return carry

    lax.fori_loop(0, n, to_device, 0)
    pltpu.make_async_copy(send_v, send_ref, sem_o).wait()


def level_kernel(n, quad, me_ref, st_ref, recv_ref, *rest):
    diag_refs, rest = rest[:2], rest[2:]
    fac_ref, dfi_ref, out_ref, diag_v, line_v, product_v, out_v, sems, sem_o = rest
    cols, deep, width = fac_ref.shape
    length = deep // width
    rows = recv_ref.shape[1]
    steps = n // quad
    me = me_ref[0]
    count = recv_ref.shape[0]
    parts = sems.shape[0]
    each = count // parts
    fetch = [
        pltpu.make_async_copy(recv_ref.at[pl.ds(i * each, each)], line_v.at[pl.ds(i * each, each)], sems.at[i]) for i in range(parts)
    ]
    for f in fetch:
        f.start()
    for a in range(2):
        for t in range(diag_refs[a].shape[0]):
            owner = lax.bitwise_xor(lax.rem(me + t % steps * quad, n), t // steps * 2 + a)
            diag_v[pl.ds(owner * rows, rows)] = diag_refs[a][t]
    ancs = [[st_ref[r, me * cols + k] for r in range(length)] for k in range(cols)]
    for f in fetch:
        f.wait()
    for k in range(cols):
        for r, anc in enumerate(ancs[k]):
            owner, local = lax.div(anc, rows), lax.rem(anc, rows)
            line = [diag_v[anc] if s == r else line_v[owner, local, s if s < r else s - 1] for s in range(length)]
            line = jnp.concatenate(line, axis=1)
            part = jnp.dot(line, fac_ref[k], preferred_element_type=jnp.float32)
            product_v[k, r * width : (r + 1) * width, :] = part.astype(jnp.bfloat16)
    for k in range(cols):
        term = lax.dot_general(fac_ref[k], product_v[k], (((0,), (0,)), ((), ())), preferred_element_type=jnp.float32)
        out_v[k] = dfi_ref[k] + term
    pltpu.make_async_copy(out_v, out_ref, sem_o).start()
    pltpu.make_async_copy(out_v, out_ref, sem_o).wait()


def shards(n, factor_blocks, inverse_blocks, diag_factor_inv, structure):
    cols, length, width, _ = factor_blocks.shape
    rows, ancestors = inverse_blocks.shape[:2]
    total = structure.shape[0]
    me = lax.axis_index("prow").astype(jnp.int32)
    me1 = me.reshape(1)
    smem = pl.BlockSpec(memory_space=pltpu.SMEM)
    vmem = pl.BlockSpec(memory_space=pltpu.VMEM)
    hbm = pl.BlockSpec(memory_space=pltpu.HBM)
    quad = 8
    steps = n // quad

    diag = pl.pallas_call(
        diag_kernel,
        out_shape=jax.ShapeDtypeStruct((1, rows, width, width), jnp.bfloat16),
        in_specs=[smem, hbm],
        out_specs=vmem,
        scratch_shapes=[pltpu.SemaphoreType.DMA((rows,))],
    )(me1, inverse_blocks)
    came = [lax.ppermute(diag, "prow", [((i + t * quad) % n, i) for i in range(n)]) for t in range(1, steps)]
    lines = -(-rows * (length - 1) // 8) * 8
    lanes = -(-n // 128) * 128
    send = pl.pallas_call(
        functools.partial(pack_kernel, n, cols),
        out_shape=jax.ShapeDtypeStruct((n, rows, length - 1, width, width), jnp.bfloat16),
        in_specs=[smem, vmem, hbm],
        out_specs=hbm,
        scratch_shapes=[
            pltpu.VMEM(inverse_blocks.shape, jnp.bfloat16),
            pltpu.VMEM((n, rows, length - 1, width, width), jnp.bfloat16),
            pltpu.VMEM((lines, lanes), jnp.int32),
            pltpu.SMEM((lines, lanes), jnp.int32),
            pltpu.SemaphoreType.DMA,
            pltpu.SemaphoreType.DMA,
            pltpu.SemaphoreType.DMA,
        ],
        compiler_params=pltpu.CompilerParams(vmem_limit_bytes=56 * 2**20),
    )(me1, structure.T, inverse_blocks)
    send, *came = lax.optimization_barrier((send, *came))
    recv = lax.all_to_all(send, "prow", split_axis=0, concat_axis=0, tiled=True)
    held = [diag] + came
    held = jnp.concatenate(held, axis=0)
    pair = jnp.concatenate([held, lax.ppermute(held, "prow", [(i ^ 2, i) for i in range(n)])], axis=0)
    chips = [pair, lax.ppermute(pair, "prow", [(i ^ 4, i) for i in range(n)])]
    chips = jnp.concatenate(chips, axis=0)
    spread = [chips, lax.ppermute(chips, "prow", [(i ^ 1, i) for i in range(n)])]
    deep = length * width
    return pl.pallas_call(
        functools.partial(level_kernel, n, quad),
        out_shape=jax.ShapeDtypeStruct((cols, width, width), jnp.float32),
        in_specs=[smem, smem, hbm] + [vmem] * 4,
        out_specs=hbm,
        scratch_shapes=[
            pltpu.VMEM((ancestors, width, width), jnp.bfloat16),
            pltpu.VMEM(recv.shape, jnp.bfloat16),
            pltpu.VMEM((cols, deep, width), jnp.bfloat16),
            pltpu.VMEM((cols, width, width), jnp.float32),
            pltpu.SemaphoreType.DMA((8,)),
            pltpu.SemaphoreType.DMA,
        ],
        compiler_params=pltpu.CompilerParams(vmem_limit_bytes=51 * 2**20),
    )(me1, structure.T, recv, *spread, factor_blocks.reshape(cols, deep, width), diag_factor_inv)


def solution(mesh):
    placed = (
        P(("pole", "prow"), None, None, None),
        P(("pole", "prow"), None, None, None),
        P(("pole", "prow"), None, None),
        P(),
    )
    return jax.shard_map(
        functools.partial(shards, mesh.shape["prow"]),
        mesh=mesh,
        in_specs=placed,
        out_specs=P(("pole", "prow"), None, None),
        check_vma=False,
    )
```

```python
import functools

import jax
import jax.numpy as jnp
from jax import lax
from jax.experimental import pallas as pl
from jax.experimental.pallas import tpu as pltpu
from jax.sharding import PartitionSpec as P


def diag_kernel(me_ref, inv_ref, diag_ref, sem):
    rows = inv_ref.shape[0]
    for j in range(rows):
        pltpu.make_async_copy(inv_ref.at[j, me_ref[0] * rows + j], diag_ref.at[0, j], sem.at[j]).start()
    for j in range(rows):
        pltpu.make_async_copy(inv_ref.at[j, 0], diag_ref.at[0, j], sem.at[j]).wait()


def pack_kernel(n, cols, me_ref, st_ref, inv_ref, send_ref, inv_v, send_v, idx_v, idx_s, sem, sem_i, sem_o):
    length, total = st_ref.shape
    rows = inv_ref.shape[0]
    others = length - 1
    me = me_ref[0]
    fetch = pltpu.make_async_copy(inv_ref, inv_v, sem)
    fetch.start()
    st = [st_ref[r : r + 1, :] for r in range(length)]
    lines = []
    for j in range(rows):
        row = me * rows + j
        for q in range(others):
            line = jnp.zeros((1, total), jnp.int32)
            for r in range(length):
                line = jnp.where(st[r] == row, st[q if q < r else q + 1], line)
            lines.append(line)
    lines.append(jnp.zeros((idx_v.shape[0] - len(lines), total), jnp.int32))
    picks = jnp.concatenate(lines, axis=0).astype(jnp.float32)
    grid = (total, idx_v.shape[1])
    first = lax.broadcasted_iota(jnp.int32, grid, 1) * cols
    place = lax.broadcasted_iota(jnp.int32, grid, 0)
    group = ((place >= first) & (place < first + cols)).astype(jnp.float32)
    table = jnp.dot(picks, group, preferred_element_type=jnp.float32, precision=lax.Precision.HIGHEST)
    idx_v[...] = table.astype(jnp.int32)
    copy = pltpu.make_async_copy(idx_v, idx_s, sem_i)
    copy.start()
    copy.wait()
    fetch.wait()

    def to_device(p, carry):
        for j in range(rows):
            for q in range(others):
                send_v[p, j, q] = inv_v[j, idx_s[j * others + q, p]]
        pltpu.make_async_copy(send_v.at[p], send_ref.at[p], sem_o).start()
        return carry

    lax.fori_loop(0, n, to_device, 0)
    pltpu.make_async_copy(send_v, send_ref, sem_o).wait()


def level_kernel(n, quad, me_ref, st_ref, recv_ref, *rest):
    diag_refs, rest = rest[:2], rest[2:]
    fac_ref, dfi_ref, out_ref, diag_v, line_v, product_v, out_v, where_s, sems, sem_o = rest
    cols, width, _ = dfi_ref.shape
    length = fac_ref.shape[0] // cols
    ancestors = diag_v.shape[0]
    rows = recv_ref.shape[1]
    steps = n // quad
    me = me_ref[0]
    count = recv_ref.shape[0]
    parts = sems.shape[0]
    each = count // parts
    fetch = [
        pltpu.make_async_copy(recv_ref.at[pl.ds(i * each, each)], line_v.at[pl.ds(i * each, each)], sems.at[i]) for i in range(parts)
    ]
    for f in fetch:
        f.start()
    if ancestors > cols * length:

        def no_place(i, carry):
            where_s[i] = cols * length
            return carry

        lax.fori_loop(0, ancestors, no_place, 0)
    for k in range(cols):
        for r in range(length):
            where_s[st_ref[r, me * cols + k]] = k * length + r
    for a in range(2):
        for t in range(diag_refs[a].shape[0]):
            owner = lax.bitwise_xor(lax.rem(me + t % steps * quad, n), t // steps * 2 + a)
            diag_v[pl.ds(owner * rows, rows)] = diag_refs[a][t]
    for i, f in enumerate(fetch):
        f.wait()
        for owner in range(i * each, (i + 1) * each):
            for j in range(rows):
                anc = owner * rows + j
                at = where_s[anc]
                own = lax.min(at, cols * length - 1)
                r = lax.rem(own, length)
                mates = [own - r + q + (q >= r).astype(jnp.int32) for q in range(length - 1)]
                line = jnp.concatenate([line_v[owner, j, q] for q in range(length - 1)] + [diag_v[anc]], axis=1)
                facs = jnp.concatenate([fac_ref[at_q] for at_q in mates + [own]], axis=0)
                part = jnp.dot(line, facs, preferred_element_type=jnp.float32)
                product_v[at] = part.astype(jnp.bfloat16)
    for k in range(cols):
        blocks = pl.ds(k * length, length)
        fac, product = fac_ref[blocks].reshape(length * width, width), product_v[blocks].reshape(length * width, width)
        term = lax.dot_general(fac, product, (((0,), (0,)), ((), ())), preferred_element_type=jnp.float32)
        out_v[k] = dfi_ref[k] + term
    pltpu.make_async_copy(out_v, out_ref, sem_o).start()
    pltpu.make_async_copy(out_v, out_ref, sem_o).wait()


def shards(n, factor_blocks, inverse_blocks, diag_factor_inv, structure):
    cols, length, width, _ = factor_blocks.shape
    rows, ancestors = inverse_blocks.shape[:2]
    total = structure.shape[0]
    me = lax.axis_index("prow").astype(jnp.int32)
    me1 = me.reshape(1)
    smem = pl.BlockSpec(memory_space=pltpu.SMEM)
    vmem = pl.BlockSpec(memory_space=pltpu.VMEM)
    hbm = pl.BlockSpec(memory_space=pltpu.HBM)
    quad = 8
    steps = n // quad

    diag = pl.pallas_call(
        diag_kernel,
        out_shape=jax.ShapeDtypeStruct((1, rows, width, width), jnp.bfloat16),
        in_specs=[smem, hbm],
        out_specs=vmem,
        scratch_shapes=[pltpu.SemaphoreType.DMA((rows,))],
    )(me1, inverse_blocks)
    came = [lax.ppermute(diag, "prow", [((i + t * quad) % n, i) for i in range(n)]) for t in range(1, steps)]
    lines = -(-rows * (length - 1) // 8) * 8
    lanes = -(-n // 128) * 128
    send = pl.pallas_call(
        functools.partial(pack_kernel, n, cols),
        out_shape=jax.ShapeDtypeStruct((n, rows, length - 1, width, width), jnp.bfloat16),
        in_specs=[smem, vmem, hbm],
        out_specs=hbm,
        scratch_shapes=[
            pltpu.VMEM(inverse_blocks.shape, jnp.bfloat16),
            pltpu.VMEM((n, rows, length - 1, width, width), jnp.bfloat16),
            pltpu.VMEM((lines, lanes), jnp.int32),
            pltpu.SMEM((lines, lanes), jnp.int32),
            pltpu.SemaphoreType.DMA,
            pltpu.SemaphoreType.DMA,
            pltpu.SemaphoreType.DMA,
        ],
        compiler_params=pltpu.CompilerParams(vmem_limit_bytes=56 * 2**20),
    )(me1, structure.T, inverse_blocks)
    send, *came = lax.optimization_barrier((send, *came))
    recv = lax.all_to_all(send, "prow", split_axis=0, concat_axis=0, tiled=True)
    held = [diag] + came
    held = jnp.concatenate(held, axis=0)
    pair = jnp.concatenate([held, lax.ppermute(held, "prow", [(i ^ 2, i) for i in range(n)])], axis=0)
    chips = [pair, lax.ppermute(pair, "prow", [(i ^ 4, i) for i in range(n)])]
    chips = jnp.concatenate(chips, axis=0)
    spread = [chips, lax.ppermute(chips, "prow", [(i ^ 1, i) for i in range(n)])]
    deep = length * width
    return pl.pallas_call(
        functools.partial(level_kernel, n, quad),
        out_shape=jax.ShapeDtypeStruct((cols, width, width), jnp.float32),
        in_specs=[smem, smem, hbm] + [vmem] * 4,
        out_specs=hbm,
        scratch_shapes=[
            pltpu.VMEM((ancestors, width, width), jnp.bfloat16),
            pltpu.VMEM(recv.shape, jnp.bfloat16),
            pltpu.VMEM((cols * length + 1, width, width), jnp.bfloat16),
            pltpu.VMEM((cols, width, width), jnp.float32),
            pltpu.SMEM((ancestors,), jnp.int32),
            pltpu.SemaphoreType.DMA((4,)),
            pltpu.SemaphoreType.DMA,
        ],
        compiler_params=pltpu.CompilerParams(vmem_limit_bytes=51 * 2**20),
    )(me1, structure.T, recv, *spread, factor_blocks.reshape(cols * length, width, width), diag_factor_inv)


def solution(mesh):
    placed = (
        P(("pole", "prow"), None, None, None),
        P(("pole", "prow"), None, None, None),
        P(("pole", "prow"), None, None),
        P(),
    )
    return jax.shard_map(
        functools.partial(shards, mesh.shape["prow"]),
        mesh=mesh,
        in_specs=placed,
        out_specs=P(("pole", "prow"), None, None),
        check_vma=False,
    )
```

```python
import functools

import jax
import jax.numpy as jnp
from jax import lax
from jax.experimental import pallas as pl
from jax.experimental.pallas import tpu as pltpu
from jax.sharding import PartitionSpec as P


def diag_kernel(me_ref, inv_ref, diag_ref, sem):
    rows = inv_ref.shape[0]
    for j in range(rows):
        pltpu.make_async_copy(inv_ref.at[j, me_ref[0] * rows + j], diag_ref.at[0, j], sem.at[j]).start()
    for j in range(rows):
        pltpu.make_async_copy(inv_ref.at[j, 0], diag_ref.at[0, j], sem.at[j]).wait()


def pack_kernel(n, cols, me_ref, st_ref, inv_ref, send_ref, inv_v, send_v, idx_v, idx_s, sem, sem_i, sem_o):
    length, total = st_ref.shape
    rows = inv_ref.shape[0]
    others = length - 1
    me = me_ref[0]
    fetch = pltpu.make_async_copy(inv_ref, inv_v, sem)
    fetch.start()
    st = [st_ref[r : r + 1, :] for r in range(length)]
    lines = []
    for j in range(rows):
        row = me * rows + j
        for q in range(others):
            line = jnp.zeros((1, total), jnp.int32)
            for r in range(length):
                line = jnp.where(st[r] == row, st[q if q < r else q + 1], line)
            lines.append(line)
    lines.append(jnp.zeros((idx_v.shape[0] - len(lines), total), jnp.int32))
    picks = jnp.concatenate(lines, axis=0).astype(jnp.float32)
    grid = (total, idx_v.shape[1])
    first = lax.broadcasted_iota(jnp.int32, grid, 1) * cols
    place = lax.broadcasted_iota(jnp.int32, grid, 0)
    group = ((place >= first) & (place < first + cols)).astype(jnp.float32)
    table = jnp.dot(picks, group, preferred_element_type=jnp.float32, precision=lax.Precision.HIGHEST)
    idx_v[...] = table.astype(jnp.int32)
    copy = pltpu.make_async_copy(idx_v, idx_s, sem_i)
    copy.start()
    copy.wait()
    fetch.wait()

    def to_device(p, carry):
        for j in range(rows):
            for q in range(others):
                send_v[p, j, q] = inv_v[j, idx_s[j * others + q, p]]
        pltpu.make_async_copy(send_v.at[p], send_ref.at[p], sem_o).start()
        return carry

    lax.fori_loop(0, n, to_device, 0)
    pltpu.make_async_copy(send_v, send_ref, sem_o).wait()


def level_kernel(n, quad, me_ref, st_ref, recv_ref, *rest):
    diag_refs, rest = rest[:2], rest[2:]
    fac_ref, dfi_ref, out_ref, diag_v, line_v, product_v, out_v, where_s, sems, sem_o = rest
    cols, width, _ = dfi_ref.shape
    length = fac_ref.shape[0] // cols
    ancestors = diag_v.shape[0]
    rows = recv_ref.shape[1]
    steps = n // quad
    me = me_ref[0]
    count = recv_ref.shape[0]
    parts = sems.shape[0]
    each = count // parts
    fetch = [
        pltpu.make_async_copy(recv_ref.at[pl.ds(i * each, each)], line_v.at[pl.ds(i * each, each)], sems.at[i]) for i in range(parts)
    ]
    for f in fetch:
        f.start()
    if ancestors > cols * length:

        def no_place(i, carry):
            where_s[i] = cols * length
            return carry

        lax.fori_loop(0, ancestors, no_place, 0)
    for k in range(cols):
        for r in range(length):
            where_s[st_ref[r, me * cols + k]] = k * length + r
    for a in range(2):
        for t in range(diag_refs[a].shape[0]):
            owner = lax.bitwise_xor(lax.rem(me + t % steps * quad, n), t // steps * 2 + a)
            diag_v[pl.ds(owner * rows, rows)] = diag_refs[a][t]
    for i, f in enumerate(fetch):
        f.wait()
        for owner in range(i * each, (i + 1) * each):
            for j in range(rows):
                anc = owner * rows + j
                at = where_s[anc]
                own = lax.min(at, cols * length - 1)
                r = lax.rem(own, length)
                mates = [own - r + q + (q >= r).astype(jnp.int32) for q in range(length - 1)]
                line = jnp.concatenate([line_v[owner, j, q] for q in range(length - 1)] + [diag_v[anc]], axis=1)
                facs = jnp.concatenate([fac_ref[at_q] for at_q in mates + [own]], axis=0)
                part = jnp.dot(line, facs, preferred_element_type=jnp.float32)
                product_v[at] = part.astype(jnp.bfloat16)
    for k in range(cols):
        blocks = pl.ds(k * length, length)
        fac, product = fac_ref[blocks].reshape(length * width, width), product_v[blocks].reshape(length * width, width)
        term = lax.dot_general(fac, product, (((0,), (0,)), ((), ())), preferred_element_type=jnp.float32)
        out_v[k] = dfi_ref[k] + term
    pltpu.make_async_copy(out_v, out_ref, sem_o).start()
    pltpu.make_async_copy(out_v, out_ref, sem_o).wait()


def shards(n, factor_blocks, inverse_blocks, diag_factor_inv, structure):
    cols, length, width, _ = factor_blocks.shape
    rows, ancestors = inverse_blocks.shape[:2]
    total = structure.shape[0]
    me = lax.axis_index("prow").astype(jnp.int32)
    me1 = me.reshape(1)
    smem = pl.BlockSpec(memory_space=pltpu.SMEM)
    vmem = pl.BlockSpec(memory_space=pltpu.VMEM)
    hbm = pl.BlockSpec(memory_space=pltpu.HBM)
    quad = 8
    steps = n // quad

    diag = pl.pallas_call(
        diag_kernel,
        out_shape=jax.ShapeDtypeStruct((1, rows, width, width), jnp.bfloat16),
        in_specs=[smem, hbm],
        out_specs=vmem,
        scratch_shapes=[pltpu.SemaphoreType.DMA((rows,))],
    )(me1, inverse_blocks)
    came = [lax.ppermute(diag, "prow", [((i + t * quad) % n, i) for i in range(n)]) for t in range(1, steps)]
    lines = -(-rows * (length - 1) // 8) * 8
    lanes = -(-n // 128) * 128
    send = pl.pallas_call(
        functools.partial(pack_kernel, n, cols),
        out_shape=jax.ShapeDtypeStruct((n, rows, length - 1, width, width), jnp.bfloat16),
        in_specs=[smem, vmem, hbm],
        out_specs=hbm,
        scratch_shapes=[
            pltpu.VMEM(inverse_blocks.shape, jnp.bfloat16),
            pltpu.VMEM((n, rows, length - 1, width, width), jnp.bfloat16),
            pltpu.VMEM((lines, lanes), jnp.int32),
            pltpu.SMEM((lines, lanes), jnp.int32),
            pltpu.SemaphoreType.DMA,
            pltpu.SemaphoreType.DMA,
            pltpu.SemaphoreType.DMA,
        ],
        compiler_params=pltpu.CompilerParams(vmem_limit_bytes=56 * 2**20),
    )(me1, structure.T, inverse_blocks)
    send, *came = lax.optimization_barrier((send, *came))
    recv = lax.all_to_all(send, "prow", split_axis=0, concat_axis=0, tiled=True)
    held = [diag] + came
    held = jnp.concatenate(held, axis=0)
    pair = jnp.concatenate([held, lax.ppermute(held, "prow", [(i ^ 2, i) for i in range(n)])], axis=0)
    chips = [pair, lax.ppermute(pair, "prow", [(i ^ 4, i) for i in range(n)])]
    chips = jnp.concatenate(chips, axis=0)
    spread = [chips, lax.ppermute(chips, "prow", [(i ^ 1, i) for i in range(n)])]
    deep = length * width
    return pl.pallas_call(
        functools.partial(level_kernel, n, quad),
        out_shape=jax.ShapeDtypeStruct((cols, width, width), jnp.float32),
        in_specs=[smem, smem, hbm] + [vmem] * 4,
        out_specs=hbm,
        scratch_shapes=[
            pltpu.VMEM((ancestors, width, width), jnp.bfloat16),
            pltpu.VMEM(recv.shape, jnp.bfloat16),
            pltpu.VMEM((cols * length + 1, width, width), jnp.bfloat16),
            pltpu.VMEM((cols, width, width), jnp.float32),
            pltpu.SMEM((ancestors,), jnp.int32),
            pltpu.SemaphoreType.DMA((2,)),
            pltpu.SemaphoreType.DMA,
        ],
        compiler_params=pltpu.CompilerParams(vmem_limit_bytes=51 * 2**20),
    )(me1, structure.T, recv, *spread, factor_blocks.reshape(cols * length, width, width), diag_factor_inv)


def solution(mesh):
    placed = (
        P(("pole", "prow"), None, None, None),
        P(("pole", "prow"), None, None, None),
        P(("pole", "prow"), None, None),
        P(),
    )
    return jax.shard_map(
        functools.partial(shards, mesh.shape["prow"]),
        mesh=mesh,
        in_specs=placed,
        out_specs=P(("pole", "prow"), None, None),
        check_vma=False,
    )
```
